32 devices in a mesh: groups: 1, expert: 8 (over z, y), dp: 4 (over x, core).
Axes of the slice: x: 2, y: 2, z: 4, core: 2. Of those that a mesh axis runs over, the one named last changes fastest.
Arguments:
- tokens: bfloat16 [4096, 2048], P(('groups', 'expert', 'dp')), may hold values from -6 to 6
- expert_ids: int32 [4096, 10], P(('groups', 'expert', 'dp')), may hold values from 0 to 31, all different within a row; in each aligned block of 128 rows (0 to 127, 128 to 255, ...) at most 48 rows name the same one
- route_weight: bfloat16 [4096, 10], P(('groups', 'expert', 'dp')), may hold values from 0.019897461 to 0.29882812
- expert_gate: bfloat16 [32, 2048, 512], P(('expert', 'dp')), may hold values from -0.125 to 0.125
- expert_up: bfloat16 [32, 2048, 512], P(('expert', 'dp')), may hold values from -0.125 to 0.125
- expert_down: bfloat16 [32, 512, 2048], P(('expert', 'dp')), may hold values from -0.25 to 0.25
- shared_gate_up: bfloat16 [2048, 1024], P('dp'), may hold values from -0.125 to 0.125
- shared_down: bfloat16 [512, 2048], P(None, 'dp'), may hold values from -0.25 to 0.25
- shared_switch: bfloat16 [2048], replicated, may hold values from -0.125 to 0.125
Outputs:
- mixed: bfloat16 [4096, 2048], P(('groups', 'expert', 'dp'))
The draws below stay inside these ranges and needn't reach their ends.
Inputs may be any that keep to these rules, and one draw needn't show every extreme that they name: `expert_ids`: each row names 10 different experts. Within the 128 rows of one device no expert is named by more than 48 rows, and in some device's rows one expert is named exactly 48 times.
All inputs are finite; a program needn't handle non-finite values.
Results may differ from the reference program's by a relative error of at most 0.0053.
Values may be sent and summed in bfloat16 or wider, within the bound.
No kernel may reach another device: no remote copies, remote signals or barrier semaphores. Data moves between devices by JAX's collectives and lax.ppermute only.
A program may use at most 128 MiB of HBM per device.

```python
import math
import jax
import jax.numpy as jnp
import numpy as np
from jax import lax

D = 2048
FF = 512
SFF = 512
TOP = 10
TOK_DEV = 128
EXPERTS = 32
CAP = 48
ROWS_EXP = 1536
TOKENS = 4096


def steps_of(stream_key, shape, cuts, smallest, largest):
    factor_of, own = 1.0, jax.random.fold_in(stream_key, 6)
    for dim, parts in cuts:
        draws = jnp.exp(jax.random.uniform(jax.random.fold_in(own, dim), (parts,), jnp.float32, smallest / len(cuts), largest / len(cuts)))
        factor_of = factor_of * jnp.repeat(draws, shape[dim] // parts).reshape([-1 if axis == dim else 1 for axis in range(len(shape))])
    return factor_of


def assign_block(rng, own, number, rows, count, top, reach, lean):
    ranking = jax.random.permutation(rng, count)
    crowded, ordinary = load_shares(count, rows * top, reach, lean, True), load_shares(count, rows * top, reach, lean, False)
    places = jnp.arange(count)

    def named(tallies, offset_by):
        used = int((tallies > 0).sum())
        fixed = max(1, used // 4)
        shifted = fixed + (places - fixed + offset_by * (used - fixed)) % max(1, count - fixed)
        return jnp.zeros((count,), jnp.int32).at[ranking[jnp.where(places < fixed, places, shifted)]].set(jnp.asarray(tallies, jnp.int32))

    tallies = jnp.where(number % 4 == 0, named(crowded, number // 4), named(ordinary, number - number // 4 - 1))
    mixed = jax.random.permutation(jax.random.fold_in(own, 3), count)
    donor, taker = mixed[0:count // 2 * 2:2], mixed[1:count // 2 * 2:2]
    margin = jnp.minimum(tallies[donor] - 1, reach - tallies[taker]) // 2
    margin = jnp.where((donor == ranking[0]) | (taker == ranking[0]) | (tallies[taker] == 0), 0, jnp.maximum(margin, 0))
    shifted = jax.random.randint(jax.random.fold_in(own, 4), (count // 2,), 0, 1 << 20) % (margin + 1)
    tallies = tallies.at[donor].add(-shifted).at[taker].add(shifted)
    items = jnp.searchsorted(jnp.cumsum(tallies), jnp.arange(rows * top), side="right").astype(jnp.int32)
    grid = items.reshape(top, rows).T
    grid = grid[jax.random.permutation(jax.random.fold_in(own, 1), rows)]
    offset_by = jax.random.randint(jax.random.fold_in(own, 2), (rows, 1), 0, top)
    return jnp.take_along_axis(grid, (jnp.arange(top)[None, :] + offset_by) % top, axis=1)


def load_shares(count, total, bound, slope, full):
    loads = [(1 << 20) // math.isqrt(standing ** slope) + 1 for standing in range(1, count + 1)]
    largest = bound if full else min(bound, max(-(-total // count), total * loads[0] // sum(loads)))
    least = 1 if total - largest >= count - 1 else 0
    given, surplus = [largest] + [least] * (count - 1), total - largest - least * (count - 1)
    while surplus > 0:
        free = [i for i in range(1, count) if given[i] < largest] or [i for i in range(1, count) if given[i] < bound]
        pool, remaining = sum([loads[i] for i in free]), surplus
        for i in free:
            addition = min(bound - given[i], max(1, remaining * loads[i] // pool), surplus)
            given[i] = given[i] + addition
            surplus = surplus - addition
    return np.array(given)


def scatter_about(stream_key, shape, deviation, reach, split=(), kind=jnp.bfloat16):
    entries = deviation * jax.random.normal(stream_key, shape, jnp.float32)
    if split:
        entries = entries * steps_of(stream_key, shape, split, -0.22, 0.18)
    return jnp.clip(entries, -reach, reach).astype(kind)


def setup_inputs(seed: int = 0, part: int = 0) -> dict:
    splits = jax.random.split(jax.random.key(seed), 10)
    own_keys = jax.random.split(jax.random.fold_in(splits[9], part), 10)
    tokens = scatter_about(own_keys[0], (TOKENS, D), 1.0, 6.0, ((0, 32),))
    expert_ids_keys = jax.random.split(jax.random.fold_in(own_keys[1], 1), TOKENS // TOK_DEV)
    expert_ids_turns = jax.random.permutation(jax.random.fold_in(own_keys[1], 3), TOKENS // TOK_DEV)
    expert_ids = jax.vmap(lambda own, number: assign_block(jax.random.fold_in(own_keys[1], 2), own, number, TOK_DEV, EXPERTS, TOP, CAP, 2))(expert_ids_keys, expert_ids_turns).reshape((TOKENS, TOP))
    route_weight = jnp.clip(jnp.exp(math.log(0.29882812) - 2.7092764 * jax.random.uniform(own_keys[2], (TOKENS, TOP), jnp.float32) ** steps_of(own_keys[2], (TOKENS, TOP), ((0, 32),), -0.2, 0.2)), 0.019897461, 0.29882812).astype(jnp.bfloat16)
    expert_gate = scatter_about(splits[3], (EXPERTS, D, FF), D ** -0.5, 0.125, ((0, 32),))
    expert_up = scatter_about(splits[4], (EXPERTS, D, FF), D ** -0.5, 0.125, ((0, 32),))
    expert_down = scatter_about(splits[5], (EXPERTS, FF, D), FF ** -0.5, 0.25, ((0, 32),))
    shared_gate_up = scatter_about(splits[6], (D, 2 * SFF), D ** -0.5, 0.125, ((0, 4),))
    shared_down = scatter_about(splits[7], (SFF, D), SFF ** -0.5, 0.25, ((1, 4),))
    shared_switch = scatter_about(splits[8], (D,), D ** -0.5, 0.125)
    return {"tokens": tokens, "expert_ids": expert_ids, "route_weight": route_weight, "expert_gate": expert_gate, "expert_up": expert_up, "expert_down": expert_down, "shared_gate_up": shared_gate_up, "shared_down": shared_down, "shared_switch": shared_switch}


def reference(tokens, expert_ids, route_weight, expert_gate, expert_up, expert_down, shared_gate_up, shared_down, shared_switch):
    flat_ids = expert_ids.reshape(-1).astype(jnp.int32)
    flat_weight = route_weight.reshape(-1)
    assign_count = flat_ids.shape[0]

    def one_expert(expert, routed):
        chosen = jnp.nonzero(flat_ids == expert, size=ROWS_EXP, fill_value=assign_count)[0].astype(jnp.int32)
        valid = chosen < assign_count
        picked = jnp.minimum(chosen, assign_count - 1)
        token_index = picked // TOP
        inputs = tokens[token_index]
        gate = jnp.dot(inputs, expert_gate[expert], preferred_element_type=jnp.float32)
        upper = jnp.dot(inputs, expert_up[expert], preferred_element_type=jnp.float32)
        hidden = (jax.nn.silu(gate) * upper).astype(jnp.bfloat16)
        answer = jnp.dot(hidden, expert_down[expert], preferred_element_type=jnp.float32)
        answer = (answer * flat_weight[picked].astype(jnp.float32)[:, None]).astype(jnp.bfloat16)
        added = jnp.where(valid[:, None], answer.astype(jnp.float32), jnp.float32(0.0))
        return routed.at[token_index].add(added)

    routed = lax.fori_loop(0, EXPERTS, one_expert, jnp.zeros(tokens.shape, jnp.float32))
    both = jnp.dot(tokens, shared_gate_up, preferred_element_type=jnp.float32)
    shared_hidden = (jax.nn.silu(both[:, :SFF]) * both[:, SFF:]).astype(jnp.bfloat16)
    shared_out = jnp.dot(shared_hidden, shared_down, preferred_element_type=jnp.float32)
    switch = jax.nn.sigmoid(jnp.dot(tokens, shared_switch, preferred_element_type=jnp.float32))
    return (routed + switch[:, None] * shared_out).astype(jnp.bfloat16)
```

```python
import jax
import jax.numpy as jnp
from jax import lax
from jax.sharding import PartitionSpec as P

BOTH = ("expert", "dp")
RING = (0, 1, 3, 2)


def moved(array, step):
    pairs = []
    for device in range(32):
        z, y, x, core = device // 8, device // 4 % 2, device // 2 % 2, device % 2
        z, y, x, core = step(z, y, x, core)
        pairs.append((device, ((z * 2 + y) * 2 + x) * 2 + core))
    return lax.ppermute(array, BOTH, pairs)


def to_core(z, y, x, core):
    return z, y, x, 1 - core


def to_x(z, y, x, core):
    return z, y, 1 - x, core


def to_y(z, y, x, core):
    return z, 1 - y, x, core


def ring_on(z, y, x, core):
    return RING[(RING.index(z) + 1) % 4], y, x, core


def ring_back(z, y, x, core):
    return RING[(RING.index(z) + 3) % 4], y, x, core


def blocks(
    tokens,
    expert_ids,
    route_weight,
    expert_gate,
    expert_up,
    expert_down,
    shared_gate_up,
    shared_down,
    shared_switch,
):
    bf16, f32 = jnp.bfloat16, jnp.float32
    rows, width = tokens.shape
    half = rows // 2
    me = lax.axis_index(BOTH)
    z, y, x, core = me // 8, me // 4 % 2, me // 2 % 2, me % 2
    ring_place = jnp.array(RING)[z]

    dense = jnp.sum(
        jnp.where(
            expert_ids.T[:, None, :] == jnp.arange(32, dtype=jnp.int32)[None, :, None],
            route_weight.T[:, None, :].astype(f32),
            0.0,
        ),
        axis=0,
    ).astype(bf16)
    pairs = jnp.broadcast_to(dense.reshape(16, 1, 2 * rows), (16, 2, 2 * rows)).reshape(32, 1, 2 * rows)
    got = lax.all_to_all(pairs, BOTH, split_axis=0, concat_axis=0, tiled=True).reshape(32, 2 * rows)
    sources = []
    for back in range(4):
        for dy in range(2):
            for dx in range(2):
                from_z = jnp.array(RING)[(ring_place + 4 - back) % 4]
                sources.append(((from_z * 2 + (y + dy) % 2) * 2 + (x + dx) % 2) * 2 + core)
    pick = (jnp.stack(sources)[:, None] == jnp.arange(32)[None, :]).astype(bf16)
    slot_weight = jnp.dot(pick, got, preferred_element_type=f32)
    slot_weight = slot_weight.reshape(4, 4, 2, rows).transpose(0, 2, 1, 3).reshape(4, 2, 4 * rows, 1)

    mine = (expert_gate[0], expert_up[0], expert_down[0])
    other = tuple(moved(part, to_core) for part in mine)
    my_weight = jnp.where(core == 0, slot_weight[:, 0], slot_weight[:, 1])
    other_weight = jnp.where(core == 0, slot_weight[:, 1], slot_weight[:, 0])

    feature = shared_gate_up.shape[1] // 8
    group = jnp.stack([shared_gate_up[:, q * feature : (q + 1) * feature] for q in range(8)])

    def plane_slice(y_to, x_to):
        q = y_to * 2 + x_to
        gate_part = lax.dynamic_index_in_dim(group, q, 0, keepdims=False)
        up_part = lax.dynamic_index_in_dim(group, 4 + q, 0, keepdims=False)
        down_part = lax.dynamic_slice_in_dim(shared_down, q * feature, feature, 0)
        return jnp.concatenate([gate_part, up_part], axis=1), down_part

    own_up, own_down = plane_slice(y, x)
    sent_up, sent_down = plane_slice(y, 1 - x)
    far_up, far_down = moved(sent_up, to_x), moved(sent_down, to_x)
    near_up2, near_down2 = moved(own_up, to_core), moved(own_down, to_core)
    far_up2, far_down2 = moved(far_up, to_core), moved(far_down, to_core)
    def by_k(own, near, far, far_near):
        low = jnp.where(core == 0, jnp.stack([own, near]), jnp.stack([near, own]))
        high = jnp.where(core == 0, jnp.stack([far, far_near]), jnp.stack([far_near, far]))
        return jnp.where(x == 0, jnp.stack([low, high]), jnp.stack([high, low]))

    shared_in = by_k(own_up, near_up2, far_up, far_up2).reshape(width, 2 * feature)
    shared_out_rows = by_k(own_down, near_down2, far_down, far_down2)
    shared_out_rows = shared_out_rows.transpose(2, 0, 1, 3).reshape(feature, width)

    columns = [tokens]
    for back in range(3):
        columns.append(moved(columns[-1], ring_on))
    partial = []
    for back in range(4):
        block = columns[back]
        by_x, by_y = moved(block, to_x), moved(block, to_y)
        corner_top = moved(by_y[:half], to_x)
        corner_low = moved(by_x[half:], to_y)
        stacked = jnp.concatenate([block, by_x, by_y, corner_top, corner_low], axis=0)
        total = 0.0
        for part, weight in ((mine, my_weight[back]), (other, other_weight[back])):
            gate = jnp.dot(stacked, part[0], preferred_element_type=f32)
            upper = jnp.dot(stacked, part[1], preferred_element_type=f32)
            hidden = (jax.nn.silu(gate) * upper).astype(bf16)
            total = total + jnp.dot(hidden, part[2], preferred_element_type=f32) * weight
        if back == 0:
            both = jnp.dot(stacked, shared_in, preferred_element_type=f32)
            hidden = (jax.nn.silu(both[:, :feature]) * both[:, feature:]).astype(bf16)
            switch = jax.nn.sigmoid(jnp.dot(stacked, shared_switch, preferred_element_type=f32))
            total = total + switch[:, None] * jnp.dot(hidden, shared_out_rows, preferred_element_type=f32)
        partial.append(total.astype(bf16).reshape(4, rows, width))

    arriving = None
    for back in (3, 2, 1, 0):
        here, along_x, along_y, corner = partial[back]
        top = moved(corner[:half], to_x).astype(f32)
        low = moved(corner[half:], to_y).astype(f32)
        along_y = jnp.concatenate([along_y[:half].astype(f32) + top, along_y[half:].astype(f32)]).astype(bf16)
        along_x = jnp.concatenate([along_x[:half].astype(f32), along_x[half:].astype(f32) + low]).astype(bf16)
        total = here.astype(f32) + moved(along_x, to_x).astype(f32) + moved(along_y, to_y).astype(f32)
        if arriving is not None:
            total = total + arriving.astype(f32)
        total = total.astype(bf16)
        if back:
            arriving = moved(total, ring_back)
    return total


def shards(
    tokens,
    expert_ids,
    route_weight,
    expert_gate,
    expert_up,
    expert_down,
    shared_gate_up,
    shared_down,
    shared_switch,
):
    tok_count, width = tokens.shape
    top_count = expert_ids.shape[1]
    device_count = lax.axis_size(("expert", "dp"))
    capacity = tok_count * top_count * 6 // (5 * device_count)
    assign_count = tok_count * top_count
    flat_ids = expert_ids.reshape(-1)
    one_hot = (flat_ids[:, None] == jnp.arange(device_count, dtype=jnp.int32)[None, :]).astype(
        jnp.int32
    )
    before = jnp.cumsum(one_hot, axis=0) - one_hot
    slot_rank = jnp.sum(before * one_hot, axis=1)
    slot_index = flat_ids * capacity + slot_rank
    filler = jnp.full((device_count * capacity,), assign_count, jnp.int32)
    owner = filler.at[slot_index].set(jnp.arange(assign_count, dtype=jnp.int32))
    filled = owner < assign_count
    picked = jnp.minimum(owner, assign_count - 1)
    outgoing = jnp.where(filled[:, None], tokens[picked // top_count], jnp.bfloat16(0.0))
    outgoing = outgoing.reshape(device_count, capacity, width)
    out_weight = jnp.where(filled, route_weight.reshape(-1)[picked], jnp.bfloat16(0.0))
    out_weight = out_weight.reshape(device_count, capacity)
    arrived = lax.all_to_all(outgoing, ("expert", "dp"), split_axis=0, concat_axis=0, tiled=True)
    shape = arrived.shape
    inputs = arrived.reshape(-1, width)
    gate = jnp.dot(inputs, expert_gate[0], preferred_element_type=jnp.float32)
    upper = jnp.dot(inputs, expert_up[0], preferred_element_type=jnp.float32)
    hidden = (jax.nn.silu(gate) * upper).astype(jnp.bfloat16)
    answer = jnp.dot(hidden, expert_down[0], preferred_element_type=jnp.float32)
    answer = answer * lax.all_to_all(
        out_weight, ("expert", "dp"), split_axis=0, concat_axis=0, tiled=True
    ).reshape(-1, 1).astype(jnp.float32)
    returned = lax.all_to_all(
        answer.astype(jnp.bfloat16).reshape(shape),
        ("expert", "dp"),
        split_axis=0,
        concat_axis=0,
        tiled=True,
    )
    returned = returned.reshape(device_count * capacity, width)
    gathered = returned[slot_index].reshape(tok_count, top_count, width)
    routed = jnp.zeros((tok_count, width), jnp.float32)
    for column in range(top_count):
        routed = routed + gathered[:, column].astype(jnp.float32)
    both = jnp.dot(
        tokens,
        lax.all_gather(shared_gate_up, "dp", axis=0, tiled=True),
        preferred_element_type=jnp.float32,
    )
    half_width = both.shape[1] // 2
    shared_hidden = (jax.nn.silu(both[:, :half_width]) * both[:, half_width:]).astype(jnp.bfloat16)
    shared_out = jnp.dot(
        shared_hidden,
        lax.all_gather(shared_down, "dp", axis=1, tiled=True),
        preferred_element_type=jnp.float32,
    )
    switch = jax.nn.sigmoid(jnp.dot(tokens, shared_switch, preferred_element_type=jnp.float32))
    return (routed + switch[:, None] * shared_out).astype(jnp.bfloat16)


def solution(mesh):
    in_specs = (
        P(("groups", "expert", "dp"), None),
        P(("groups", "expert", "dp"), None),
        P(("groups", "expert", "dp"), None),
        P(("expert", "dp"), None, None),
        P(("expert", "dp"), None, None),
        P(("expert", "dp"), None, None),
        P("dp", None),
        P(None, "dp"),
        P(),
    )
    out_specs = P(("groups", "expert", "dp"), None)
    part = blocks if (mesh.shape["expert"], mesh.shape["dp"]) == (8, 4) else shards
    return jax.shard_map(part, mesh=mesh, in_specs=in_specs, out_specs=out_specs, check_vma=False)
```

```python
import functools

import jax
import jax.numpy as jnp
from jax import lax
from jax.experimental import pallas as pl
from jax.experimental.pallas import tpu as pltpu
from jax.sharding import PartitionSpec as P

BOTH = ("expert", "dp")
bf16, f32 = jnp.bfloat16, jnp.float32


def moved(array, step):
    pairs = []
    for device in range(32):
        z, y, x, core = device // 8, device // 4 % 2, device // 2 % 2, device % 2
        z, y, x, core = step(z, y, x, core)
        pairs.append((device, ((z * 2 + y) * 2 + x) * 2 + core))
    return lax.ppermute(array, BOTH, pairs)


def to_core(z, y, x, core):
    return z, y, x, 1 - core


def to_x(z, y, x, core):
    return z, y, 1 - x, core


def to_y(z, y, x, core):
    return z, 1 - y, x, core


def ring_on(z, y, x, core):
    return (1, 3, 0, 2)[z], y, x, core


def ring_back(z, y, x, core):
    return (2, 0, 3, 1)[z], y, x, core


def silu(v):
    return v / (1.0 + jnp.exp(-v))


def prepare(ids_ref, weight_ref, up_ref, down_ref, pairs_ref, own_ref, sent_ref):
    experts = pairs_ref.shape[0]
    rows = ids_ref.shape[1]
    expert = lax.broadcasted_iota(jnp.int32, (experts, rows), 0)
    near = jnp.zeros((experts, rows), f32)
    far = jnp.zeros((experts, rows), f32)
    weights = weight_ref[...].astype(f32)
    for k in range(ids_ref.shape[0]):
        named = ids_ref[k : k + 1, :]
        weight = weights[k : k + 1, :]
        near = jnp.where(named == expert, weight, near)
        far = jnp.where((named ^ 1) == expert, weight, far)
    pairs_ref[:, :rows] = near.astype(bf16)
    pairs_ref[:, rows:] = far.astype(bf16)
    depth, both = up_ref.shape
    feature = both // 8
    half_out = down_ref.shape[1] // 2
    plane = lax.axis_index("expert") % 2 * 2
    x = lax.axis_index("dp") // 2
    for ref, place in ((own_ref, plane + x), (sent_ref, plane + 1 - x)):
        start = pl.multiple_of(place * feature, feature)
        ref[:depth, :feature] = up_ref[:, pl.ds(start, feature)]
        up_start = pl.multiple_of(both // 2 + start, feature)
        ref[:depth, feature:] = up_ref[:, pl.ds(up_start, feature)]
        for side in range(2):
            ref[depth + side * feature : depth + (side + 1) * feature, :] = down_ref[
                pl.ds(start, feature), side * half_out : (side + 1) * half_out
            ]


def feed(shared, slot, *refs):
    here, by_x, by_y, top, low = refs[:5]
    weights = refs[5:11]
    got, pick = refs[11:13]
    rest = refs[13:]
    if shared:
        pieces, switch_ref, rest = rest[:4], rest[4], rest[5:]
    out_here, out_x, out_y, out_top, out_low, rows_ref, total = rest
    step = pl.program_id(0)
    tile = here.shape[0]
    half = tile // 2

    @pl.when(step == 0)
    def _():
        rows_ref[:tile] = here[...]
        rows_ref[tile : 2 * tile] = by_x[...]
        rows_ref[2 * tile : 3 * tile] = by_y[...]
        rows_ref[3 * tile : 3 * tile + half] = top[...]
        rows_ref[3 * tile + half :] = low[...]
        if shared:
            place = lax.axis_index("dp")
            depth = rows_ref.shape[1] // 4
            feature = pieces[0].shape[1] // 2
            both = jnp.zeros((4 * tile, 2 * feature), f32)
            turn = jnp.zeros((4 * tile, 1), f32)
            for j, piece in enumerate(pieces):
                start = pl.multiple_of((place ^ j) * depth, depth)
                both += jnp.dot(rows_ref[:, pl.ds(start, depth)], piece[:depth], preferred_element_type=f32)
                fixed = slice(j * depth, (j + 1) * depth)
                turn += jnp.sum(
                    rows_ref[:, fixed].astype(f32) * switch_ref[:, fixed].astype(f32), axis=1, keepdims=True
                )
            hidden = (silu(both[:, :feature]) * both[:, feature:]).astype(bf16)
            turn = 1.0 / (1.0 + jnp.exp(-turn))
            for j, piece in enumerate(pieces):
                for side in range(2):
                    start = pl.multiple_of((place ^ j) * depth + side * (depth // 2), depth // 2)
                    part = piece[depth + side * feature : depth + (side + 1) * feature]
                    total[:, pl.ds(start, depth // 2)] = turn * jnp.dot(hidden, part, preferred_element_type=f32)
        else:
            total[...] = jnp.zeros_like(total)

    def add(gate_ref, up_ref, down_ref, which):
        columns = lax.dot_general(
            got[:, which * tile : (which + 1) * tile],
            pick[...],
            (((0,), (0,)), ((), ())),
            preferred_element_type=f32,
        )
        scale = jnp.concatenate([columns[:, slot * 4 + s : slot * 4 + s + 1] for s in range(4)], axis=0)
        gate = jnp.dot(rows_ref[...], gate_ref[0], preferred_element_type=f32)
        upper = jnp.dot(rows_ref[...], up_ref[0], preferred_element_type=f32)
        hidden = (silu(gate) * upper).astype(bf16)
        span = 512
        for start in range(0, total.shape[1], span):
            cut = slice(start, start + span)
            total[:, cut] += scale * jnp.dot(hidden, down_ref[0, :, cut], preferred_element_type=f32)

    @pl.when(step < 2)
    def _():
        add(*weights[:3], 0)

    @pl.when(step >= 2)
    def _():
        add(*weights[3:], 1)

    @pl.when(step == 3)
    def _():
        out_here[...] = total[:tile].astype(bf16)
        out_x[...] = total[tile : 2 * tile].astype(bf16)
        out_y[...] = total[2 * tile : 3 * tile].astype(bf16)
        out_top[...] = total[3 * tile : 3 * tile + half].astype(bf16)
        out_low[...] = total[3 * tile + half :].astype(bf16)


def whole(array):
    return pl.BlockSpec(array.shape, lambda i: (0,) * array.ndim)


def run_feed(slot, parts, mine, other, got, pick, extra):
    tile, width = parts[0].shape
    hidden = mine[0].shape[2]
    cut = hidden // 2

    def tiles(first):
        def at(i):
            return jnp.clip(i - first, 0, 1)

        return [
            pl.BlockSpec((1, width, cut), lambda i: (0, 0, at(i))),
            pl.BlockSpec((1, width, cut), lambda i: (0, 0, at(i))),
            pl.BlockSpec((1, cut, width), lambda i: (0, at(i), 0)),
        ]

    outs = [jax.ShapeDtypeStruct((n, width), bf16) for n in (tile, tile, tile, tile // 2, tile // 2)]
    return pl.pallas_call(
        functools.partial(feed, bool(extra), slot),
        grid=(4,),
        in_specs=[whole(p) for p in parts]
        + tiles(0)
        + tiles(2)
        + [whole(got), whole(pick)]
        + [whole(e) for e in extra],
        out_specs=[whole(o) for o in outs],
        out_shape=outs,
        scratch_shapes=[pltpu.VMEM((4 * tile, width), bf16), pltpu.VMEM((4 * tile, width), f32)],
        compiler_params=pltpu.CompilerParams(vmem_limit_bytes=40 * 1024 * 1024),
        cost_estimate=pl.CostEstimate(
            flops=2 * 4 * tile * width * hidden * 6, bytes_accessed=16 * 2**20, transcendentals=4 * tile * hidden * 2
        ),
    )(*parts, *mine, *other, got, pick, *extra)


def blocks(
    tokens,
    expert_ids,
    route_weight,
    expert_gate,
    expert_up,
    expert_down,
    shared_gate_up,
    shared_down,
    shared_switch,
):
    rows, width = tokens.shape
    half = rows // 2
    place, plane = lax.axis_index("dp"), lax.axis_index("expert")
    z, y = plane // 2, plane % 2
    ring_place = z ^ (z // 2)
    depth, both = shared_gate_up.shape
    feature = both // 8
    piece_shape = jax.ShapeDtypeStruct((depth + 2 * feature, 2 * feature), bf16)
    pairs, own, sent = pl.pallas_call(
        prepare,
        out_shape=[jax.ShapeDtypeStruct((32, 2 * rows), bf16), piece_shape, piece_shape],
    )(expert_ids.T, route_weight.T, shared_gate_up, shared_down)
    got = lax.all_to_all(pairs.reshape(32, 1, 2 * rows), BOTH, split_axis=0, concat_axis=0, tiled=True)
    got = got.reshape(32, 2 * rows)
    slot = lax.broadcasted_iota(jnp.int32, (32, 128), 1)
    from_place = (ring_place + 4 - slot // 4) % 4
    from_z = from_place ^ (from_place // 2)
    source = (from_z * 2 + (y ^ (slot // 2 % 2))) * 4 + (place ^ (slot % 2 * 2))
    pick = (source == lax.broadcasted_iota(jnp.int32, (32, 128), 0)).astype(bf16)

    mine = (expert_gate, expert_up, expert_down)
    other = tuple(moved(part, to_core) for part in mine)
    far = moved(sent, to_x)
    extra = (own, moved(own, to_core), far, moved(far, to_core), shared_switch.reshape(1, width))

    columns = [tokens]
    for back in range(3):
        columns.append(moved(columns[-1], ring_on))
    partial = []
    for back in range(4):
        block = columns[back]
        by_x, by_y = moved(block, to_x), moved(block, to_y)
        top, low = moved(by_y[:half], to_x), moved(by_x[half:], to_y)
        parts = (block, by_x, by_y, top, low)
        partial.append(run_feed(back, parts, mine, other, got, pick, () if back else extra))

    arriving = None
    for back in (3, 2, 1, 0):
        here, along_x, along_y, top, low = partial[back]
        top, low = moved(top, to_x).astype(f32), moved(low, to_y).astype(f32)
        along_y = jnp.concatenate([along_y[:half].astype(f32) + top, along_y[half:].astype(f32)]).astype(bf16)
        along_x = jnp.concatenate([along_x[:half].astype(f32), along_x[half:].astype(f32) + low]).astype(bf16)
        total = here.astype(f32) + moved(along_x, to_x).astype(f32) + moved(along_y, to_y).astype(f32)
        if arriving is not None:
            total = total + arriving.astype(f32)
        total = total.astype(bf16)
        if back:
            arriving = moved(total, ring_back)
    return total


def shards(
    tokens,
    expert_ids,
    route_weight,
    expert_gate,
    expert_up,
    expert_down,
    shared_gate_up,
    shared_down,
    shared_switch,
):
    tok_count, width = tokens.shape
    top_count = expert_ids.shape[1]
    device_count = lax.axis_size(("expert", "dp"))
    capacity = tok_count * top_count * 6 // (5 * device_count)
    assign_count = tok_count * top_count
    flat_ids = expert_ids.reshape(-1)
    one_hot = (flat_ids[:, None] == jnp.arange(device_count, dtype=jnp.int32)[None, :]).astype(
        jnp.int32
    )
    before = jnp.cumsum(one_hot, axis=0) - one_hot
    slot_rank = jnp.sum(before * one_hot, axis=1)
    slot_index = flat_ids * capacity + slot_rank
    filler = jnp.full((device_count * capacity,), assign_count, jnp.int32)
    owner = filler.at[slot_index].set(jnp.arange(assign_count, dtype=jnp.int32))
    filled = owner < assign_count
    picked = jnp.minimum(owner, assign_count - 1)
    outgoing = jnp.where(filled[:, None], tokens[picked // top_count], jnp.bfloat16(0.0))
    outgoing = outgoing.reshape(device_count, capacity, width)
    out_weight = jnp.where(filled, route_weight.reshape(-1)[picked], jnp.bfloat16(0.0))
    out_weight = out_weight.reshape(device_count, capacity)
    arrived = lax.all_to_all(outgoing, ("expert", "dp"), split_axis=0, concat_axis=0, tiled=True)
    shape = arrived.shape
    inputs = arrived.reshape(-1, width)
    gate = jnp.dot(inputs, expert_gate[0], preferred_element_type=jnp.float32)
    upper = jnp.dot(inputs, expert_up[0], preferred_element_type=jnp.float32)
    hidden = (jax.nn.silu(gate) * upper).astype(jnp.bfloat16)
    answer = jnp.dot(hidden, expert_down[0], preferred_element_type=jnp.float32)
    answer = answer * lax.all_to_all(
        out_weight, ("expert", "dp"), split_axis=0, concat_axis=0, tiled=True
    ).reshape(-1, 1).astype(jnp.float32)
    returned = lax.all_to_all(
        answer.astype(jnp.bfloat16).reshape(shape),
        ("expert", "dp"),
        split_axis=0,
        concat_axis=0,
        tiled=True,
    )
    returned = returned.reshape(device_count * capacity, width)
    gathered = returned[slot_index].reshape(tok_count, top_count, width)
    routed = jnp.zeros((tok_count, width), jnp.float32)
    for column in range(top_count):
        routed = routed + gathered[:, column].astype(jnp.float32)
    both = jnp.dot(
        tokens,
        lax.all_gather(shared_gate_up, "dp", axis=0, tiled=True),
        preferred_element_type=jnp.float32,
    )
    half_width = both.shape[1] // 2
    shared_hidden = (jax.nn.silu(both[:, :half_width]) * both[:, half_width:]).astype(jnp.bfloat16)
    shared_out = jnp.dot(
        shared_hidden,
        lax.all_gather(shared_down, "dp", axis=1, tiled=True),
        preferred_element_type=jnp.float32,
    )
    switch = jax.nn.sigmoid(jnp.dot(tokens, shared_switch, preferred_element_type=jnp.float32))
    return (routed + switch[:, None] * shared_out).astype(jnp.bfloat16)


def solution(mesh):
    in_specs = (
        P(("groups", "expert", "dp"), None),
        P(("groups", "expert", "dp"), None),
        P(("groups", "expert", "dp"), None),
        P(("expert", "dp"), None, None),
        P(("expert", "dp"), None, None),
        P(("expert", "dp"), None, None),
        P("dp", None),
        P(None, "dp"),
        P(),
    )
    out_specs = P(("groups", "expert", "dp"), None)
    part = blocks if (mesh.shape["expert"], mesh.shape["dp"]) == (8, 4) else shards
    return jax.shard_map(part, mesh=mesh, in_specs=in_specs, out_specs=out_specs, check_vma=False)
```

```python
import functools

import jax
import jax.numpy as jnp
from jax import lax
from jax.experimental import pallas as pl
from jax.experimental.pallas import tpu as pltpu
from jax.sharding import PartitionSpec as P

BOTH = ("expert", "dp")
bf16, f32 = jnp.bfloat16, jnp.float32


def moved(array, step):
    pairs = []
    for device in range(32):
        z, y, x, core = device // 8, device // 4 % 2, device // 2 % 2, device % 2
        z, y, x, core = step(z, y, x, core)
        pairs.append((device, ((z * 2 + y) * 2 + x) * 2 + core))
    return lax.ppermute(array, BOTH, pairs)


def to_x(z, y, x, core):
    return z, y, 1 - x, core


def to_y(z, y, x, core):
    return z, 1 - y, x, core


def ring_on(z, y, x, core):
    return (1, 3, 0, 2)[z], y, x, core


def ring_back(z, y, x, core):
    return (2, 0, 3, 1)[z], y, x, core


def silu(v):
    return v / (1.0 + jnp.exp(-v))


def widen(tokens_ref, ids_ref, weight_ref, wide_ref):
    rows, width = tokens_ref.shape
    wide_ref[:, :width] = tokens_ref[...]
    lanes = wide_ref.shape[1] - width
    expert = lax.broadcasted_iota(jnp.int32, (lanes, rows), 0)
    dense = jnp.zeros((lanes, rows), f32)
    weights = weight_ref[...].astype(f32)
    for k in range(ids_ref.shape[0]):
        dense = jnp.where(ids_ref[k : k + 1, :] == expert, weights[k : k + 1, :], dense)
    wide_ref[:, width:] = dense.T.astype(bf16)


def share(up_ref, down_ref, own_ref, sent_ref):
    depth, both = up_ref.shape
    feature = both // 8
    half_out = down_ref.shape[1] // 2
    plane = lax.axis_index("expert") % 2 * 2
    x = lax.axis_index("dp") // 2
    for ref, place in ((own_ref, plane + x), (sent_ref, plane + 1 - x)):
        start = pl.multiple_of(place * feature, feature)
        ref[:depth, :feature] = up_ref[:, pl.ds(start, feature)]
        up_start = pl.multiple_of(both // 2 + start, feature)
        ref[:depth, feature:] = up_ref[:, pl.ds(up_start, feature)]
        for side in range(2):
            ref[depth + side * feature : depth + (side + 1) * feature, :] = down_ref[
                pl.ds(start, feature), side * half_out : (side + 1) * half_out
            ]


def feed(shared, count, *refs):
    parts, rest = refs[:count], refs[count:]
    (gate_hbm, up_hbm, down_hbm), rest = rest[:3], rest[3:]
    if shared:
        (own, far, switch_ref), rest = rest[:3], rest[3:]
    outs, (rows_ref, scale_ref, hidden_ref, base, gate_ref, up_ref, down_ref, sems) = rest[:-8], rest[-8:]
    rows, width = rows_ref.shape
    step = pl.program_id(0)
    cut = gate_ref.shape[2]

    def tile_copies(index, which, side):
        columns = pl.ds(pl.multiple_of(side * cut, cut), cut)
        return (
            pltpu.make_async_copy(gate_hbm.at[which, 0, :, columns], gate_ref.at[index], sems.at[0, index]),
            pltpu.make_async_copy(up_hbm.at[which, 0, :, columns], up_ref.at[index], sems.at[1, index]),
        )

    def down_copies():
        return [
            pltpu.make_async_copy(down_hbm.at[which, 0], down_ref.at[which], sems.at[2, which]) for which in range(2)
        ]

    @pl.when(step == 0)
    def _():
        for index in range(4):
            for copy in tile_copies(index, index // 2, index % 2):
                copy.start()
        for copy in down_copies():
            copy.start()
        chip = lax.axis_index("expert") * 2 + lax.axis_index("dp") // 2
        start = 0
        for ref in parts:
            span = slice(start, start + ref.shape[0])
            start += ref.shape[0]
            rows_ref[span] = ref[:, :width]
            weight = ref[:, width:].astype(f32)
            expert = lax.broadcasted_iota(jnp.int32, weight.shape, 1)
            for which in range(2):
                chosen = jnp.where(expert == chip * 2 + which, weight, 0.0)
                scale_ref[which, span] = jnp.sum(chosen, axis=1, keepdims=True)
        if shared:
            x = lax.axis_index("dp") // 2
            depth = width // 4
            feature = own.shape[2] // 2
            both = jnp.zeros((rows, 2 * feature), f32)
            turn = jnp.zeros((rows, 1), f32)
            pieces = [(ref.at[core], (x ^ across) * 2 + core) for across, ref in enumerate((own, far)) for core in range(2)]
            for j, (piece, place) in enumerate(pieces):
                start = pl.multiple_of(place * depth, depth)
                both += jnp.dot(rows_ref[:, pl.ds(start, depth)], piece[:depth], preferred_element_type=f32)
                fixed = slice(j * depth, (j + 1) * depth)
                turn += jnp.sum(
                    rows_ref[:, fixed].astype(f32) * switch_ref[:, fixed].astype(f32), axis=1, keepdims=True
                )
            hidden = (silu(both[:, :feature]) * both[:, feature:]).astype(bf16)
            turn = 1.0 / (1.0 + jnp.exp(-turn))
            for piece, place in pieces:
                for side in range(2):
                    start = pl.multiple_of(place * depth + side * (depth // 2), depth // 2)
                    part = piece[depth + side * feature : depth + (side + 1) * feature]
                    base[:, pl.ds(start, depth // 2)] = turn * jnp.dot(hidden, part, preferred_element_type=f32)

    for copy in tile_copies(step, step // 2, step % 2):
        copy.wait()
    gate = jnp.dot(rows_ref[...], gate_ref[step], preferred_element_type=f32)
    upper = jnp.dot(rows_ref[...], up_ref[step], preferred_element_type=f32)
    hidden_ref[step] = (silu(gate) * upper).astype(bf16)

    @pl.when(step == 3)
    def _():
        for copy in down_copies():
            copy.wait()
        span = 512
        for start in range(0, width, span):
            columns = slice(start, start + span)
            total = base[:, columns] if shared else 0.0
            for which in range(2):
                answer = jnp.dot(hidden_ref[2 * which], down_ref[which, :cut, columns], preferred_element_type=f32)
                answer += jnp.dot(hidden_ref[2 * which + 1], down_ref[which, cut:, columns], preferred_element_type=f32)
                total = total + scale_ref[which] * answer
            total = total.astype(bf16)
            first = 0
            for ref in outs:
                ref[:, columns] = total[first : first + ref.shape[0]]
                first += ref.shape[0]


def whole(array):
    return pl.BlockSpec(array.shape, lambda i: (0,) * array.ndim)


def run_feed(parts, cuts, experts, extra):
    hidden, width = experts[2].shape[2:]
    rows, cut = sum(cuts), hidden // 2
    outs = [jax.ShapeDtypeStruct((n, width), bf16) for n in cuts]
    return pl.pallas_call(
        functools.partial(feed, bool(extra), len(parts)),
        grid=(4,),
        in_specs=[whole(p) for p in parts]
        + [pl.BlockSpec(memory_space=pltpu.HBM)] * 3
        + [whole(e) for e in extra],
        out_specs=[whole(o) for o in outs],
        out_shape=outs,
        scratch_shapes=[
            pltpu.VMEM((rows, width), bf16),
            pltpu.VMEM((2, rows, 1), f32),
            pltpu.VMEM((4, rows, cut), bf16),
            pltpu.VMEM((rows, width) if extra else (8, 128), f32),
            pltpu.VMEM((4, width, cut), bf16),
            pltpu.VMEM((4, width, cut), bf16),
            pltpu.VMEM((2, hidden, width), bf16),
            pltpu.SemaphoreType.DMA((3, 4)),
        ],
        compiler_params=pltpu.CompilerParams(vmem_limit_bytes=28 * 1024 * 1024),
        cost_estimate=pl.CostEstimate(
            flops=2 * rows * width * hidden * 6, bytes_accessed=16 * 2**20, transcendentals=rows * hidden * 2
        ),
    )(*parts, *experts, *extra)


def summed(*terms):
    return sum(term.astype(f32) for term in terms).astype(bf16)


def top_added(array, top):
    half = top.shape[0]
    return jnp.concatenate([array[:half].astype(f32) + top.astype(f32), array[half:].astype(f32)]).astype(bf16)


def low_added(array, low):
    half = low.shape[0]
    return jnp.concatenate([array[:half].astype(f32), array[half:].astype(f32) + low.astype(f32)]).astype(bf16)


def blocks(
    tokens,
    expert_ids,
    route_weight,
    expert_gate,
    expert_up,
    expert_down,
    shared_gate_up,
    shared_down,
    shared_switch,
):
    rows, width = tokens.shape
    half = rows // 2
    depth, both = shared_gate_up.shape
    feature = both // 8
    wide = pl.pallas_call(
        widen,
        out_shape=jax.ShapeDtypeStruct((rows, width + 128), bf16),
    )(tokens, expert_ids.T, route_weight.T)
    piece_shape = jax.ShapeDtypeStruct((depth + 2 * feature, 2 * feature), bf16)
    own, sent = pl.pallas_call(share, out_shape=[piece_shape, piece_shape])(shared_gate_up, shared_down)
    cores = [[0, 1], [2, 3]]

    def paired(part):
        return lax.all_gather(part, "dp", axis_index_groups=cores)

    experts = [paired(part) for part in (expert_gate, expert_up, expert_down)]
    on_x = on_y = on_z = moved

    first = on_z(wide, ring_on)
    x0, y0 = on_x(wide, to_x), on_y(wide, to_y)
    second = on_z(first, ring_on)
    top, low = on_x(y0[:half], to_x), on_y(x0[half:], to_y)
    corner0 = jnp.concatenate([top, low])
    x1, y1 = on_x(first, to_x), on_y(first, to_y)
    corner1 = on_z(corner0, ring_on)
    third = on_z(wide, ring_back)
    x2, y2 = on_x(second, to_x), on_y(second, to_y)
    corner2 = on_z(corner1, ring_on)
    far = on_x(sent, to_x)
    x3, y3 = on_x(third, to_x), on_y(third, to_y)
    top, low = on_x(y3[:half], to_x), on_y(x3[half:], to_y)
    full, halves = (rows,) * 4, (rows,) * 3 + (half,) * 2
    partial1 = run_feed((first, x1, y1, corner1), full, experts, ())
    partial2 = run_feed((second, x2, y2, corner2), halves, experts, ())
    partial3 = run_feed((third, x3, y3, top, low), halves, experts, ())
    extra = (paired(own), paired(far), shared_switch.reshape(1, width))
    partial0 = run_feed((wide, x0, y0, corner0), full, experts, extra)

    def straight(here, along_x, along_y):
        return here, on_x(along_x, to_x), on_y(along_y, to_y)

    def in_plane(here, along_x, along_y, top, low):
        top, low = on_x(top, to_x), on_y(low, to_y)
        return straight(here, low_added(along_x, low), top_added(along_y, top))

    plane1 = straight(*partial1[:3])
    corner = on_z(partial1[3], ring_back)
    plane2 = in_plane(*partial2)
    second = on_z(summed(*plane2), ring_back)
    plane3 = in_plane(*partial3)
    first = on_z(summed(*plane1, second), ring_back)
    third = on_z(summed(*plane3), ring_on)
    corner = summed(partial0[3], corner)
    plane0 = in_plane(*partial0[:3], corner[:half], corner[half:])
    return summed(*plane0, first, third)


def shards(
    tokens,
    expert_ids,
    route_weight,
    expert_gate,
    expert_up,
    expert_down,
    shared_gate_up,
    shared_down,
    shared_switch,
):
    tok_count, width = tokens.shape
    top_count = expert_ids.shape[1]
    device_count = lax.axis_size(("expert", "dp"))
    capacity = tok_count * top_count * 6 // (5 * device_count)
    assign_count = tok_count * top_count
    flat_ids = expert_ids.reshape(-1)
    one_hot = (flat_ids[:, None] == jnp.arange(device_count, dtype=jnp.int32)[None, :]).astype(
        jnp.int32
    )
    before = jnp.cumsum(one_hot, axis=0) - one_hot
    slot_rank = jnp.sum(before * one_hot, axis=1)
    slot_index = flat_ids * capacity + slot_rank
    filler = jnp.full((device_count * capacity,), assign_count, jnp.int32)
    owner = filler.at[slot_index].set(jnp.arange(assign_count, dtype=jnp.int32))
    filled = owner < assign_count
    picked = jnp.minimum(owner, assign_count - 1)
    outgoing = jnp.where(filled[:, None], tokens[picked // top_count], jnp.bfloat16(0.0))
    outgoing = outgoing.reshape(device_count, capacity, width)
    out_weight = jnp.where(filled, route_weight.reshape(-1)[picked], jnp.bfloat16(0.0))
    out_weight = out_weight.reshape(device_count, capacity)
    arrived = lax.all_to_all(outgoing, ("expert", "dp"), split_axis=0, concat_axis=0, tiled=True)
    shape = arrived.shape
    inputs = arrived.reshape(-1, width)
    gate = jnp.dot(inputs, expert_gate[0], preferred_element_type=jnp.float32)
    upper = jnp.dot(inputs, expert_up[0], preferred_element_type=jnp.float32)
    hidden = (jax.nn.silu(gate) * upper).astype(jnp.bfloat16)
    answer = jnp.dot(hidden, expert_down[0], preferred_element_type=jnp.float32)
    answer = answer * lax.all_to_all(
        out_weight, ("expert", "dp"), split_axis=0, concat_axis=0, tiled=True
    ).reshape(-1, 1).astype(jnp.float32)
    returned = lax.all_to_all(
        answer.astype(jnp.bfloat16).reshape(shape),
        ("expert", "dp"),
        split_axis=0,
        concat_axis=0,
        tiled=True,
    )
    returned = returned.reshape(device_count * capacity, width)
    gathered = returned[slot_index].reshape(tok_count, top_count, width)
    routed = jnp.zeros((tok_count, width), jnp.float32)
    for column in range(top_count):
        routed = routed + gathered[:, column].astype(jnp.float32)
    both = jnp.dot(
        tokens,
        lax.all_gather(shared_gate_up, "dp", axis=0, tiled=True),
        preferred_element_type=jnp.float32,
    )
    half_width = both.shape[1] // 2
    shared_hidden = (jax.nn.silu(both[:, :half_width]) * both[:, half_width:]).astype(jnp.bfloat16)
    shared_out = jnp.dot(
        shared_hidden,
        lax.all_gather(shared_down, "dp", axis=1, tiled=True),
        preferred_element_type=jnp.float32,
    )
    switch = jax.nn.sigmoid(jnp.dot(tokens, shared_switch, preferred_element_type=jnp.float32))
    return (routed + switch[:, None] * shared_out).astype(jnp.bfloat16)


def solution(mesh):
    in_specs = (
        P(("groups", "expert", "dp"), None),
        P(("groups", "expert", "dp"), None),
        P(("groups", "expert", "dp"), None),
        P(("expert", "dp"), None, None),
        P(("expert", "dp"), None, None),
        P(("expert", "dp"), None, None),
        P("dp", None),
        P(None, "dp"),
        P(),
    )
    out_specs = P(("groups", "expert", "dp"), None)
    part = blocks if (mesh.shape["expert"], mesh.shape["dp"]) == (8, 4) else shards
    return jax.shard_map(part, mesh=mesh, in_specs=in_specs, out_specs=out_specs, check_vma=False)
```

```python
import functools

import jax
import jax.numpy as jnp
from jax import lax
from jax.experimental import pallas as pl
from jax.experimental.pallas import tpu as pltpu
from jax.sharding import PartitionSpec as P

BOTH = ("expert", "dp")
bf16, f32 = jnp.bfloat16, jnp.float32


def moved(array, step):
    pairs = []
    for device in range(32):
        z, y, x, core = device // 8, device // 4 % 2, device // 2 % 2, device % 2
        z, y, x, core = step(z, y, x, core)
        pairs.append((device, ((z * 2 + y) * 2 + x) * 2 + core))
    return lax.ppermute(array, BOTH, pairs)


def ordered(array, *done):
    return lax.optimization_barrier((array, *done))[0] if done else array


def to_x(z, y, x, core):
    return z, y, 1 - x, core


def to_y(z, y, x, core):
    return z, 1 - y, x, core


def ring_on(z, y, x, core):
    return (1, 3, 0, 2)[z], y, x, core


def ring_back(z, y, x, core):
    return (2, 0, 3, 1)[z], y, x, core


def silu(v):
    return v / (1.0 + jnp.exp(-v))


def widen(tokens_ref, ids_ref, weight_ref, wide_ref):
    rows, width = tokens_ref.shape
    wide_ref[:, :width] = tokens_ref[...]
    lanes = wide_ref.shape[1] - width
    expert = lax.broadcasted_iota(jnp.int32, (lanes, rows), 0)
    dense = jnp.zeros((lanes, rows), f32)
    weights = weight_ref[...].astype(f32)
    for k in range(ids_ref.shape[0]):
        dense = jnp.where(ids_ref[k : k + 1, :] == expert, weights[k : k + 1, :], dense)
    wide_ref[:, width:] = dense.T.astype(bf16)


def share(up_ref, down_ref, own_ref, sent_ref):
    depth, both = up_ref.shape
    feature = both // 8
    half_out = down_ref.shape[1] // 2
    plane = lax.axis_index("expert") % 2 * 2
    x = lax.axis_index("dp") // 2
    for ref, place in ((own_ref, plane + x), (sent_ref, plane + 1 - x)):
        start = pl.multiple_of(place * feature, feature)
        ref[:depth, :feature] = up_ref[:, pl.ds(start, feature)]
        up_start = pl.multiple_of(both // 2 + start, feature)
        ref[:depth, feature:] = up_ref[:, pl.ds(up_start, feature)]
        for side in range(2):
            ref[depth + side * feature : depth + (side + 1) * feature, :] = down_ref[
                pl.ds(start, feature), side * half_out : (side + 1) * half_out
            ]


def feed(shared, count, *refs):
    parts, rest = refs[:count], refs[count:]
    (gate_hbm, up_hbm, down_hbm), rest = rest[:3], rest[3:]
    if shared:
        (own, far, switch_ref), rest = rest[:3], rest[3:]
    outs, (rows_ref, scale_ref, hidden_ref, base, gate_ref, up_ref, down_ref, sems) = rest[:-8], rest[-8:]
    rows, width = rows_ref.shape
    step = pl.program_id(0)
    cut = gate_ref.shape[2]

    def tile_copies(index, which, side):
        columns = pl.ds(pl.multiple_of(side * cut, cut), cut)
        return (
            pltpu.make_async_copy(gate_hbm.at[which, 0, :, columns], gate_ref.at[index], sems.at[0, index]),
            pltpu.make_async_copy(up_hbm.at[which, 0, :, columns], up_ref.at[index], sems.at[1, index]),
        )

    def down_copies():
        return [
            pltpu.make_async_copy(down_hbm.at[which, 0], down_ref.at[which], sems.at[2, which]) for which in range(2)
        ]

    @pl.when(step == 0)
    def _():
        for index in range(4):
            for copy in tile_copies(index, index // 2, index % 2):
                copy.start()
        for copy in down_copies():
            copy.start()
        chip = lax.axis_index("expert") * 2 + lax.axis_index("dp") // 2
        start = 0
        for ref in parts:
            span = slice(start, start + ref.shape[0])
            start += ref.shape[0]
            rows_ref[span] = ref[:, :width]
            weight = ref[:, width:].astype(f32)
            expert = lax.broadcasted_iota(jnp.int32, weight.shape, 1)
            for which in range(2):
                chosen = jnp.where(expert == chip * 2 + which, weight, 0.0)
                scale_ref[which, span] = jnp.sum(chosen, axis=1, keepdims=True)
        if shared:
            x = lax.axis_index("dp") // 2
            depth = width // 4
            feature = own.shape[2] // 2
            both = jnp.zeros((rows, 2 * feature), f32)
            turn = jnp.zeros((rows, 1), f32)
            pieces = [(ref.at[core], (x ^ across) * 2 + core) for across, ref in enumerate((own, far)) for core in range(2)]
            for j, (piece, place) in enumerate(pieces):
                start = pl.multiple_of(place * depth, depth)
                both += jnp.dot(rows_ref[:, pl.ds(start, depth)], piece[:depth], preferred_element_type=f32)
                fixed = slice(j * depth, (j + 1) * depth)
                turn += jnp.sum(
                    rows_ref[:, fixed].astype(f32) * switch_ref[:, fixed].astype(f32), axis=1, keepdims=True
                )
            hidden = (silu(both[:, :feature]) * both[:, feature:]).astype(bf16)
            turn = 1.0 / (1.0 + jnp.exp(-turn))
            for piece, place in pieces:
                for side in range(2):
                    start = pl.multiple_of(place * depth + side * (depth // 2), depth // 2)
                    part = piece[depth + side * feature : depth + (side + 1) * feature]
                    base[:, pl.ds(start, depth // 2)] = turn * jnp.dot(hidden, part, preferred_element_type=f32)

    for copy in tile_copies(step, step // 2, step % 2):
        copy.wait()
    gate = jnp.dot(rows_ref[...], gate_ref[step], preferred_element_type=f32)
    upper = jnp.dot(rows_ref[...], up_ref[step], preferred_element_type=f32)
    hidden_ref[step] = (silu(gate) * upper).astype(bf16)

    @pl.when(step == 3)
    def _():
        for copy in down_copies():
            copy.wait()
        span = 512
        for start in range(0, width, span):
            columns = slice(start, start + span)
            total = base[:, columns] if shared else 0.0
            for which in range(2):
                answer = jnp.dot(hidden_ref[2 * which], down_ref[which, :cut, columns], preferred_element_type=f32)
                answer += jnp.dot(hidden_ref[2 * which + 1], down_ref[which, cut:, columns], preferred_element_type=f32)
                total = total + scale_ref[which] * answer
            total = total.astype(bf16)
            first = 0
            for ref in outs:
                ref[:, columns] = total[first : first + ref.shape[0]]
                first += ref.shape[0]


def whole(array):
    return pl.BlockSpec(array.shape, lambda i: (0,) * array.ndim)


def run_feed(parts, cuts, experts, extra):
    hidden, width = experts[2].shape[2:]
    rows, cut = sum(cuts), hidden // 2
    outs = [jax.ShapeDtypeStruct((n, width), bf16) for n in cuts]
    return pl.pallas_call(
        functools.partial(feed, bool(extra), len(parts)),
        grid=(4,),
        in_specs=[whole(p) for p in parts]
        + [pl.BlockSpec(memory_space=pltpu.HBM)] * 3
        + [whole(e) for e in extra],
        out_specs=[whole(o) for o in outs],
        out_shape=outs,
        scratch_shapes=[
            pltpu.VMEM((rows, width), bf16),
            pltpu.VMEM((2, rows, 1), f32),
            pltpu.VMEM((4, rows, cut), bf16),
            pltpu.VMEM((rows, width) if extra else (8, 128), f32),
            pltpu.VMEM((4, width, cut), bf16),
            pltpu.VMEM((4, width, cut), bf16),
            pltpu.VMEM((2, hidden, width), bf16),
            pltpu.SemaphoreType.DMA((3, 4)),
        ],
        compiler_params=pltpu.CompilerParams(vmem_limit_bytes=40 * 1024 * 1024),
        cost_estimate=pl.CostEstimate(
            flops=2 * rows * width * hidden * 6, bytes_accessed=16 * 2**20, transcendentals=rows * hidden * 2
        ),
    )(*parts, *experts, *extra)


def summed(*terms):
    return sum(term.astype(f32) for term in terms).astype(bf16)


def top_added(array, top):
    half = top.shape[0]
    return jnp.concatenate([array[:half].astype(f32) + top.astype(f32), array[half:].astype(f32)]).astype(bf16)


def low_added(array, low):
    half = low.shape[0]
    return jnp.concatenate([array[:half].astype(f32), array[half:].astype(f32) + low.astype(f32)]).astype(bf16)


def blocks(
    tokens,
    expert_ids,
    route_weight,
    expert_gate,
    expert_up,
    expert_down,
    shared_gate_up,
    shared_down,
    shared_switch,
):
    rows, width = tokens.shape
    half = rows // 2
    depth, both = shared_gate_up.shape
    feature = both // 8
    wide = pl.pallas_call(
        widen,
        out_shape=jax.ShapeDtypeStruct((rows, width + 128), bf16),
    )(tokens, expert_ids.T, route_weight.T)
    piece_shape = jax.ShapeDtypeStruct((depth + 2 * feature, 2 * feature), bf16)
    own, sent = pl.pallas_call(share, out_shape=[piece_shape, piece_shape])(shared_gate_up, shared_down)
    cores = [[0, 1], [2, 3]]

    def paired(part):
        return lax.all_gather(part, "dp", axis_index_groups=cores)

    experts = [paired(part) for part in (expert_gate, expert_up, expert_down)]
    on_x = on_y = on_z = moved

    first = on_z(wide, ring_on)
    x0, y0 = on_x(wide, to_x), on_y(wide, to_y)
    second = on_z(first, ring_on)
    top, low = on_x(y0[:half], to_x), on_y(x0[half:], to_y)
    corner0 = jnp.concatenate([top, low])
    x1, y1 = on_x(first, to_x), on_y(first, to_y)
    corner1 = on_z(corner0, ring_on)
    third = on_z(wide, ring_back)
    x2, y2 = on_x(ordered(second, *experts), to_x), on_y(second, to_y)
    corner2 = on_z(corner1, ring_on)
    far = on_x(sent, to_x)
    x3, y3 = on_x(third, to_x), on_y(third, to_y)
    top, low = on_x(y3[:half], to_x), on_y(x3[half:], to_y)
    full, halves = (rows,) * 4, (rows,) * 3 + (half,) * 2

    def straight(here, along_x, along_y):
        return here, on_x(along_x, to_x), on_y(along_y, to_y)

    def corners(top, low):
        return on_x(top, to_x), on_y(low, to_y)

    def in_plane(here, along_x, along_y, top, low):
        return straight(here, low_added(along_x, low), top_added(along_y, top))

    partial1 = run_feed((first, x1, y1, corner1), full, experts, ())
    plane1 = straight(*ordered(partial1[:3], x2, y2))
    corner = on_z(partial1[3], ring_back)
    partial2 = run_feed((second, x2, y2, corner2), halves, experts, ())
    ends2 = corners(*partial2[3:])
    partial3 = run_feed((ordered(third, *plane1[1:]), x3, y3, top, low), halves, experts, ())
    plane2 = in_plane(*partial2[:3], *ends2)
    second = on_z(summed(*plane2), ring_back)
    ends3 = corners(*partial3[3:])
    extra = (paired(own), paired(far), shared_switch.reshape(1, width))
    partial0 = run_feed((ordered(wide, *ends2), x0, y0, corner0), full, experts, extra)
    plane3 = in_plane(*partial3[:3], *ends3)
    first = on_z(summed(*plane1, second), ring_back)
    third = on_z(summed(*plane3), ring_on)
    corner = summed(partial0[3], corner)
    ends0 = corners(corner[:half], corner[half:])
    plane0 = in_plane(*partial0[:3], *ends0)
    return summed(*plane0, first, third)


def shards(
    tokens,
    expert_ids,
    route_weight,
    expert_gate,
    expert_up,
    expert_down,
    shared_gate_up,
    shared_down,
    shared_switch,
):
    tok_count, width = tokens.shape
    top_count = expert_ids.shape[1]
    device_count = lax.axis_size(("expert", "dp"))
    capacity = tok_count * top_count * 6 // (5 * device_count)
    assign_count = tok_count * top_count
    flat_ids = expert_ids.reshape(-1)
    one_hot = (flat_ids[:, None] == jnp.arange(device_count, dtype=jnp.int32)[None, :]).astype(
        jnp.int32
    )
    before = jnp.cumsum(one_hot, axis=0) - one_hot
    slot_rank = jnp.sum(before * one_hot, axis=1)
    slot_index = flat_ids * capacity + slot_rank
    filler = jnp.full((device_count * capacity,), assign_count, jnp.int32)
    owner = filler.at[slot_index].set(jnp.arange(assign_count, dtype=jnp.int32))
    filled = owner < assign_count
    picked = jnp.minimum(owner, assign_count - 1)
    outgoing = jnp.where(filled[:, None], tokens[picked // top_count], jnp.bfloat16(0.0))
    outgoing = outgoing.reshape(device_count, capacity, width)
    out_weight = jnp.where(filled, route_weight.reshape(-1)[picked], jnp.bfloat16(0.0))
    out_weight = out_weight.reshape(device_count, capacity)
    arrived = lax.all_to_all(outgoing, ("expert", "dp"), split_axis=0, concat_axis=0, tiled=True)
    shape = arrived.shape
    inputs = arrived.reshape(-1, width)
    gate = jnp.dot(inputs, expert_gate[0], preferred_element_type=jnp.float32)
    upper = jnp.dot(inputs, expert_up[0], preferred_element_type=jnp.float32)
    hidden = (jax.nn.silu(gate) * upper).astype(jnp.bfloat16)
    answer = jnp.dot(hidden, expert_down[0], preferred_element_type=jnp.float32)
    answer = answer * lax.all_to_all(
        out_weight, ("expert", "dp"), split_axis=0, concat_axis=0, tiled=True
    ).reshape(-1, 1).astype(jnp.float32)
    returned = lax.all_to_all(
        answer.astype(jnp.bfloat16).reshape(shape),
        ("expert", "dp"),
        split_axis=0,
        concat_axis=0,
        tiled=True,
    )
    returned = returned.reshape(device_count * capacity, width)
    gathered = returned[slot_index].reshape(tok_count, top_count, width)
    routed = jnp.zeros((tok_count, width), jnp.float32)
    for column in range(top_count):
        routed = routed + gathered[:, column].astype(jnp.float32)
    both = jnp.dot(
        tokens,
        lax.all_gather(shared_gate_up, "dp", axis=0, tiled=True),
        preferred_element_type=jnp.float32,
    )
    half_width = both.shape[1] // 2
    shared_hidden = (jax.nn.silu(both[:, :half_width]) * both[:, half_width:]).astype(jnp.bfloat16)
    shared_out = jnp.dot(
        shared_hidden,
        lax.all_gather(shared_down, "dp", axis=1, tiled=True),
        preferred_element_type=jnp.float32,
    )
    switch = jax.nn.sigmoid(jnp.dot(tokens, shared_switch, preferred_element_type=jnp.float32))
    return (routed + switch[:, None] * shared_out).astype(jnp.bfloat16)


def solution(mesh):
    in_specs = (
        P(("groups", "expert", "dp"), None),
        P(("groups", "expert", "dp"), None),
        P(("groups", "expert", "dp"), None),
        P(("expert", "dp"), None, None),
        P(("expert", "dp"), None, None),
        P(("expert", "dp"), None, None),
        P("dp", None),
        P(None, "dp"),
        P(),
    )
    out_specs = P(("groups", "expert", "dp"), None)
    part = blocks if (mesh.shape["expert"], mesh.shape["dp"]) == (8, 4) else shards
    return jax.shard_map(part, mesh=mesh, in_specs=in_specs, out_specs=out_specs, check_vma=False)
```
